32 devices in a mesh: dp: 8 (over z, x), seq: 4 (over y, core).
Axes of the slice: x: 2, y: 2, z: 4, core: 2. Of those that a mesh axis runs over, the one named last changes fastest.
Arguments:
- tokens: bfloat16 [16, 1536, 960], P('dp', 'seq'), may hold values from -6 to 6
- cotangent: bfloat16 [16, 1536, 960], P('dp', 'seq'), may hold values from -6 to 6
- wq: bfloat16 [960, 960], P('dp', 'seq'), may hold values from -0.1875 to 0.1875
- wk: bfloat16 [960, 320], P('dp', 'seq'), may hold values from -0.1875 to 0.1875
- wv: bfloat16 [960, 320], P('dp', 'seq'), may hold values from -0.1875 to 0.1875
- wo: bfloat16 [960, 960], P('dp', 'seq'), may hold values from -1 to 1
- w_gate: bfloat16 [960, 2560], P('dp', 'seq'), may hold values from -0.1875 to 0.1875
- w_up: bfloat16 [960, 2560], P('dp', 'seq'), may hold values from -0.1875 to 0.1875
- w_down: bfloat16 [2560, 960], P('dp', 'seq'), may hold values from -0.125 to 0.125
- gains: bfloat16 [2, 960], P(None, 'dp'), may hold values from 0.5 to 1.5
Outputs:
- block_out: bfloat16 [16, 1536, 960], P('dp', 'seq')
- grad_tokens: bfloat16 [16, 1536, 960], P('dp', 'seq')
- grad_wq: float32 [960, 960], P('dp', 'seq')
- grad_wk: float32 [960, 320], P('dp', 'seq')
- grad_wv: float32 [960, 320], P('dp', 'seq')
- grad_wo: float32 [960, 960], P('dp', 'seq')
- grad_w_gate: float32 [960, 2560], P('dp', 'seq')
- grad_w_up: float32 [960, 2560], P('dp', 'seq')
- grad_w_down: float32 [2560, 960], P('dp', 'seq')
- grad_gains: float32 [2, 960], P(None, 'dp')
The draws below stay inside these ranges and needn't reach their ends.
All inputs are finite; a program needn't handle non-finite values.
Results may differ from the reference program's by a relative error of at most 0.018.
Values may be sent and summed in bfloat16 or wider, within the bound.
A program may use at most 256 MiB of HBM per device.

```python
import jax
import jax.numpy as jnp
from jax import lax

MODEL_WIDTH = 960
QUERY_HEADS = 15
KEY_VALUE_HEADS = 5
HEAD_SIZE = 64
FF = 2560
SEQUENCE_LENGTH = 1536
NSEQ = 16


def levels(rng, extent, pieces, low, high):
    def one(position, shards_of):
        heights = jax.random.uniform(jax.random.fold_in(jax.random.fold_in(rng, 6), position), (shards_of,), jnp.float32, low / len(pieces), high / len(pieces))
        return jnp.repeat(jnp.exp(heights), extent[position] // shards_of).reshape((-1,) + (1,) * (len(extent) - position - 1))

    loudness = one(*pieces[0])
    for cut in pieces[1:]:
        loudness = loudness * one(*cut)
    return loudness


def gaussian(rng, shape, scale, most, shards=(), held_as=jnp.bfloat16):
    factor_of = levels(rng, shape, shards, -0.22, 0.18) if shards else 1.0
    array = jax.random.normal(rng, shape, jnp.float32) * scale * factor_of
    return jnp.minimum(jnp.maximum(array, -most), most).astype(held_as)


def setup_inputs(seed: int = 0) -> dict:
    splits = jax.random.split(jax.random.key(seed), 11)
    tokens = gaussian(splits[0], (NSEQ, SEQUENCE_LENGTH, MODEL_WIDTH), 1.0, 6.0, ((0, 8), (1, 4)))
    cotangent = gaussian(splits[1], (NSEQ, SEQUENCE_LENGTH, MODEL_WIDTH), 1.0, 6.0, ((0, 8), (1, 4)))
    wq = gaussian(splits[2], (MODEL_WIDTH, QUERY_HEADS * HEAD_SIZE), MODEL_WIDTH ** -0.5, 0.1875, ((0, 8), (1, 4)))
    wk = gaussian(splits[3], (MODEL_WIDTH, KEY_VALUE_HEADS * HEAD_SIZE), MODEL_WIDTH ** -0.5, 0.1875, ((0, 8), (1, 4)))
    wv = gaussian(splits[4], (MODEL_WIDTH, KEY_VALUE_HEADS * HEAD_SIZE), MODEL_WIDTH ** -0.5, 0.1875, ((0, 8), (1, 4)))
    wo = gaussian(splits[5], (QUERY_HEADS * HEAD_SIZE, MODEL_WIDTH), (HEAD_SIZE // 2) ** -0.5, 1.0, ((0, 8), (1, 4)))
    w_gate = gaussian(splits[6], (MODEL_WIDTH, FF), MODEL_WIDTH ** -0.5, 0.1875, ((0, 8), (1, 4)))
    w_up = gaussian(splits[7], (MODEL_WIDTH, FF), MODEL_WIDTH ** -0.5, 0.1875, ((0, 8), (1, 4)))
    w_down = gaussian(splits[8], (FF, MODEL_WIDTH), FF ** -0.5, 0.125, ((0, 8), (1, 4)))
    gains = jnp.clip(1.0 + 0.1 * jax.random.normal(splits[9], (2, MODEL_WIDTH), jnp.float32), 0.5, 1.5).astype(jnp.bfloat16)
    return dict(tokens=tokens, cotangent=cotangent, wq=wq, wk=wk, wv=wv, wo=wo, w_gate=w_gate, w_up=w_up, w_down=w_down, gains=gains)


EPS = 1e-05
NEG = -1e+30
HIGH = lax.Precision.HIGHEST

@jax.custom_vjp
def reduced_precision(v):
    return lax.optimization_barrier(v.astype(jnp.bfloat16)).astype(jnp.float32)

@jax.custom_vjp
def reduced_backward(v):
    return v

def low_keep(v):
    return (reduced_precision(v), None)

def low_pass(kept, grad):
    return (grad,)

def back_keep(v):
    return (v, None)

def back_low(kept, grad):
    return (reduced_precision(grad),)
reduced_precision.defvjp(low_keep, low_pass)
reduced_backward.defvjp(back_keep, back_low)

def matrix_product(left, right):
    return jnp.dot(left, right, precision=HIGH)

def rms_scale(values, gain_row):
    return values * lax.rsqrt(lax.optimization_barrier(jnp.mean(values * values, -1, keepdims=True)) + EPS) * gain_row

def rope_tables(positions):
    half_dim = HEAD_SIZE // 2
    freq_index = jnp.arange(half_dim).astype(jnp.float32)
    inverse = 10000.0 ** (-2.0 * freq_index / HEAD_SIZE)
    angles = positions.astype(jnp.float32)[:, None] * inverse[None, :]
    return (jnp.cos(angles), jnp.sin(angles))

def apply_rotary(values, cosine_table, sine_table):
    half_dim = values.shape[-1] // 2
    first_half = values[..., :half_dim]
    second_half = values[..., half_dim:]
    cos_wide = cosine_table[:, None, :]
    sin_wide = sine_table[:, None, :]
    return jnp.concatenate([first_half * cos_wide - second_half * sin_wide, second_half * cos_wide + first_half * sin_wide], -1)

def attend(query_rotated, key_rotated, value_reduced):
    length_all = query_rotated.shape[0]
    block_rows = min(512, length_all)
    block_number = length_all // block_rows
    key_pos = jnp.arange(length_all).astype(jnp.int32)

    def block_fn(packed):
        query_blk, first_row = packed
        scores = reduced_backward(jnp.einsum('qhd,khd->hqk', query_blk, key_rotated, precision=HIGH) * 0.125)
        query_pos = first_row + jnp.arange(block_rows).astype(jnp.int32)
        visible = key_pos[None, :] <= query_pos[:, None]
        probs = jax.nn.softmax(jnp.where(visible[None], scores, NEG), axis=-1)
        return jnp.einsum('hqk,khd->qhd', reduced_precision(probs), value_reduced, precision=HIGH)
    starts = (jnp.arange(block_number) * block_rows).astype(jnp.int32)
    blocks = lax.map(jax.checkpoint(block_fn), (query_rotated.reshape(block_number, block_rows, QUERY_HEADS, HEAD_SIZE), starts))
    return blocks.reshape(length_all, QUERY_HEADS * HEAD_SIZE)

def layer(inputs, params, cosine_table, sine_table):
    q_weight, key_matrix, value_matrix, o_weight, gate_weight, up_weight, down_weight, gain_pair = params
    first_norm_output = reduced_precision(rms_scale(inputs, gain_pair[0]))
    query = reduced_backward(matrix_product(first_norm_output, q_weight)).reshape(SEQUENCE_LENGTH, QUERY_HEADS, HEAD_SIZE)
    key_projected = reduced_backward(matrix_product(first_norm_output, key_matrix)).reshape(SEQUENCE_LENGTH, KEY_VALUE_HEADS, HEAD_SIZE)
    value_reduced = reduced_precision(reduced_backward(matrix_product(first_norm_output, value_matrix))).reshape(SEQUENCE_LENGTH, KEY_VALUE_HEADS, HEAD_SIZE)
    query_rotated = reduced_precision(apply_rotary(query, cosine_table, sine_table))
    key_rotated = reduced_precision(apply_rotary(key_projected, cosine_table, sine_table))
    query_group_width = QUERY_HEADS // KEY_VALUE_HEADS
    attn = attend(query_rotated, jnp.repeat(key_rotated, query_group_width, axis=1), jnp.repeat(value_reduced, query_group_width, axis=1))
    attn_low = reduced_precision(reduced_backward(attn))
    mixed = inputs + reduced_backward(matrix_product(attn_low, o_weight))
    second_normed = reduced_precision(rms_scale(mixed, gain_pair[1]))
    gate = reduced_backward(matrix_product(second_normed, gate_weight))
    up_proj = reduced_backward(matrix_product(second_normed, up_weight))
    hidden_low = reduced_precision(jax.nn.silu(gate) * up_proj)
    return mixed + reduced_backward(matrix_product(hidden_low, down_weight))

def reference(tokens, cotangent, wq, wk, wv, wo, w_gate, w_up, w_down, gains):
    weights = (wq.astype(jnp.float32), wk.astype(jnp.float32), wv.astype(jnp.float32), wo.astype(jnp.float32), w_gate.astype(jnp.float32), w_up.astype(jnp.float32), w_down.astype(jnp.float32), gains.astype(jnp.float32))
    cosine_table, sine_table = rope_tables(jnp.arange(SEQUENCE_LENGTH).astype(jnp.int32))

    def forward(inputs, *params):
        return layer(inputs, params, cosine_table, sine_table)

    def one_sequence(totals, seq_pair):
        seq_tokens, seq_cot = seq_pair
        result, pull = jax.vjp(forward, seq_tokens.astype(jnp.float32), *weights)
        grads = pull(seq_cot.astype(jnp.float32))
        summed = tuple((running + piece_grad for running, piece_grad in zip(totals, grads[1:])))
        return (summed, (result.astype(jnp.bfloat16), grads[0].astype(jnp.bfloat16)))
    start_totals = tuple((jnp.zeros(each_weight.shape, jnp.float32) for each_weight in weights))
    totals, (outputs, grad_inputs) = lax.scan(one_sequence, start_totals, (tokens, cotangent))
    return (outputs, grad_inputs, totals[0], totals[1], totals[2], totals[3], totals[4], totals[5], totals[6], totals[7])
```

```python
import jax
import jax.numpy as jnp
from jax import lax
from jax.sharding import PartitionSpec as P

QUERY_HEADS = 15
KEY_VALUE_HEADS = 5
HEAD_SIZE = 64


EPS = 1e-05
NEG = -1e30


def bit_places():
    seq_bits = lax.axis_size("seq").bit_length() - 1
    data_bits = lax.axis_size("dp").bit_length() - 1
    return [("seq", b) for b in range(seq_bits - 1, -1, -1)] + [
        ("dp", b) for b in range(data_bits - 1, -1, -1)
    ]


def exchange(values, axis, bit):
    pairs = [(i, i ^ (1 << bit)) for i in range(lax.axis_size(axis))]
    return lax.ppermute(values, axis, pairs)


def my_bit(axis, bit):
    return (lax.axis_index(axis) >> bit) & 1


def rotated(kind):
    every = bit_places()
    seq = [p for p in every if p[0] == "seq" and p[1] > 0]
    data = [p for p in every if p[0] == "dp"]
    last = [("seq", 0)]
    if kind == 0:
        return data + seq + last
    if kind == 1:
        return data[:-1] + seq + data[-1:] + last
    return data[:-2] + seq + data[-1:] + data[-2:-1] + last


def gather_bits(shard, order, places):
    current = shard.reshape((1,) * len(places) + shard.shape)
    for axis, bit in order:
        dim = places.index((axis, bit))
        other = exchange(current, axis, bit)
        shape = [1] * current.ndim
        shape[dim] = 2
        mine = jnp.arange(2, dtype=jnp.int32).reshape(shape) == my_bit(axis, bit)
        current = jnp.where(mine, current, other)
    return current.reshape((-1,) + shard.shape)


def gather_weight(shard, kind):
    full = gather_bits(shard, rotated(kind), bit_places())
    return full.reshape(lax.axis_size("seq"), lax.axis_size("dp"), *shard.shape)


def scatter_bits(blocks, order, places):
    payload = blocks.shape[1:]
    current = blocks.reshape((2,) * len(places) + payload)
    for axis, bit in order:
        dim = places.index((axis, bit))
        here = my_bit(axis, bit)
        send = lax.dynamic_slice_in_dim(current, 1 - here, 1, dim).astype(jnp.bfloat16)
        keep = lax.dynamic_slice_in_dim(current, here, 1, dim)
        other = exchange(send, axis, bit)
        current = keep.astype(jnp.float32) + other.astype(jnp.float32)
        if (axis, bit) != order[-1]:
            current = current.astype(jnp.bfloat16)
    return current.reshape(payload)


def scatter_weight(grad, kind):
    data_ways = lax.axis_size("dp")
    seq_ways, height, breadth = grad.shape
    blocks = grad.reshape(seq_ways * data_ways, height // data_ways, breadth)
    return scatter_bits(blocks, rotated(kind)[::-1], bit_places())


def side_by_side(blocks):
    rows = blocks.reshape(blocks.shape[0], -1, blocks.shape[3])
    return jnp.concatenate([rows[i] for i in range(blocks.shape[0])], -1)


def by_columns(left, right, seq_ways):
    wide = right.shape[1] // seq_ways
    return jnp.stack(
        [
            jnp.einsum(
                "ta,tb->ab",
                left,
                right[:, i * wide : (i + 1) * wide],
                preferred_element_type=jnp.float32,
            ).astype(jnp.bfloat16)
            for i in range(seq_ways)
        ]
    )


def rope_tables(positions):
    half_dim = HEAD_SIZE // 2
    freq_index = jnp.arange(half_dim).astype(jnp.float32)
    inverse = 10000.0 ** (-2.0 * freq_index / HEAD_SIZE)
    angles = positions.astype(jnp.float32)[:, None] * inverse[None, :]
    return (jnp.cos(angles), jnp.sin(angles))


def apply_rotary(values, cosine_table, sine_table):
    half_dim = values.shape[-1] // 2
    first_half = values[..., :half_dim]
    second_half = values[..., half_dim:]
    cos_wide = cosine_table[:, None, :]
    sin_wide = sine_table[:, None, :]
    return jnp.concatenate(
        [
            first_half * cos_wide - second_half * sin_wide,
            second_half * cos_wide + first_half * sin_wide,
        ],
        -1,
    )


def inverse_rotary(grads, cosine_table, sine_table):
    half_dim = grads.shape[-1] // 2
    first_half = grads[..., :half_dim]
    second_half = grads[..., half_dim:]
    cos_wide = cosine_table[:, None, :]
    sin_wide = sine_table[:, None, :]
    return jnp.concatenate(
        [
            first_half * cos_wide + second_half * sin_wide,
            second_half * cos_wide - first_half * sin_wide,
        ],
        -1,
    )


def norm_back(grad_norm, unit, inv_rms, gain_row):
    scaled = grad_norm * gain_row
    return inv_rms * (scaled - unit * jnp.mean(scaled * unit, -1, keepdims=True))


def on_device(tokens, cotangent, wq, wk, wv, wo, w_gate, w_up, w_down, gains):
    data_ways = lax.axis_size("dp")
    seq_ways = lax.axis_size("seq")
    query_groups, slice_length, width = tokens.shape
    tok_rows = query_groups * slice_length
    query_group_width = QUERY_HEADS // KEY_VALUE_HEADS
    key_value_width = KEY_VALUE_HEADS * HEAD_SIZE
    single_float = jnp.float32
    brain_float_half = jnp.bfloat16
    seq_places = [p for p in bit_places() if p[0] == "seq"]
    shard_rows = wq.shape[0]
    qw, kw = wq.shape[1], wk.shape[1]
    packed = jnp.concatenate(
        [
            jnp.concatenate([wq, wk, wv], -1),
            jnp.pad(gains, ((0, 6), (0, qw + 2 * kw - gains.shape[1]))),
        ],
        0,
    )
    qkv_blocks = gather_weight(packed, 0)
    full_o = side_by_side(gather_weight(wo, 1))
    gate_blocks = gather_weight(w_gate, 0)
    up_blocks = gather_weight(w_up, 1)
    full_gate = side_by_side(gate_blocks)
    full_up = side_by_side(up_blocks)
    full_down = side_by_side(gather_weight(w_down, 2))
    full_q = side_by_side(qkv_blocks[:, :, :shard_rows, :qw])
    full_k = side_by_side(qkv_blocks[:, :, :shard_rows, qw : qw + kw])
    full_v = side_by_side(qkv_blocks[:, :, :shard_rows, qw + kw :])
    gain_full = (
        qkv_blocks[0, :, shard_rows : shard_rows + 2, : gains.shape[1]]
        .transpose(1, 0, 2)
        .reshape(2, width)
        .astype(single_float)
    )
    inputs = tokens.astype(single_float).reshape(tok_rows, width)
    first_rms = lax.rsqrt(jnp.mean(inputs * inputs, -1, keepdims=True) + EPS)
    first_unit = inputs * first_rms
    first_norm_output = (first_unit * gain_full[0]).astype(brain_float_half)
    query = jnp.dot(first_norm_output, full_q, preferred_element_type=single_float)
    key_projected = jnp.dot(first_norm_output, full_k, preferred_element_type=single_float)
    value_proj = jnp.dot(first_norm_output, full_v, preferred_element_type=single_float)
    positions = lax.axis_index("seq") * slice_length + jnp.arange(slice_length, dtype=jnp.int32)
    cosine_table, sine_table = rope_tables(positions)
    query_rotated = apply_rotary(
        query.reshape(query_groups, slice_length, QUERY_HEADS, HEAD_SIZE), cosine_table, sine_table
    ).astype(brain_float_half)
    key_rotated = apply_rotary(
        key_projected.reshape(query_groups, slice_length, KEY_VALUE_HEADS, HEAD_SIZE),
        cosine_table,
        sine_table,
    ).astype(brain_float_half)
    value_reduced = value_proj.astype(brain_float_half).reshape(
        query_groups, slice_length, key_value_width
    )
    key_value = jnp.concatenate(
        [key_rotated.reshape(query_groups, slice_length, key_value_width), value_reduced], -1
    )
    query_fivefold = query_rotated.reshape(
        query_groups, slice_length, KEY_VALUE_HEADS, query_group_width, HEAD_SIZE
    )
    last_pos = positions[slice_length - 1]
    statistic_shape = (query_groups, KEY_VALUE_HEADS, query_group_width, slice_length)
    start_state = (
        jnp.full(statistic_shape, NEG, single_float),
        jnp.zeros(statistic_shape, single_float),
        jnp.zeros(statistic_shape + (HEAD_SIZE,), single_float),
    )
    sequence_segment = (
        gather_bits(key_value, seq_places[::-1], seq_places)
        .transpose(1, 0, 2, 3)
        .reshape(query_groups, seq_ways * slice_length, 2 * key_value_width)
    )

    def update(state):
        best, total_sum, accum = state
        key_head_count = sequence_segment.shape[1]
        key_portion = sequence_segment[..., :key_value_width].reshape(
            query_groups, key_head_count, KEY_VALUE_HEADS, HEAD_SIZE
        )
        value_portion = sequence_segment[..., key_value_width:].reshape(
            query_groups, key_head_count, KEY_VALUE_HEADS, HEAD_SIZE
        )
        scores = (
            jnp.einsum(
                "sqkgd,sjkd->skgqj",
                query_fivefold,
                key_portion,
                preferred_element_type=single_float,
            )
            * 0.125
        )
        visible = jnp.arange(key_head_count, dtype=jnp.int32)[None, :] <= positions[:, None]
        scores = jnp.where(visible, scores, NEG)
        new_best = jnp.maximum(best, jnp.max(scores, -1))
        weights_exp = jnp.exp(scores - new_best[..., None])
        total_sum = jnp.sum(weights_exp, -1)
        accum = jnp.einsum(
            "skgqj,sjkd->skgqd",
            weights_exp.astype(brain_float_half),
            value_portion,
            preferred_element_type=single_float,
        )
        return (new_best, total_sum, accum)

    best, total_sum, accum = lax.cond(
        jnp.int32(0) <= last_pos, update, lambda state: state, start_state
    )
    log_total = best + jnp.log(total_sum)
    attn_nat = (accum / total_sum[..., None]).transpose(0, 3, 1, 2, 4)
    attn_low = attn_nat.reshape(tok_rows, QUERY_HEADS * HEAD_SIZE).astype(brain_float_half)
    mixed = inputs + jnp.dot(attn_low, full_o, preferred_element_type=single_float)
    second_rms = lax.rsqrt(jnp.mean(mixed * mixed, -1, keepdims=True) + EPS)
    second_unit = mixed * second_rms
    second_normed = (second_unit * gain_full[1]).astype(brain_float_half)
    gate = jnp.dot(second_normed, full_gate, preferred_element_type=single_float)
    up_proj = jnp.dot(second_normed, full_up, preferred_element_type=single_float)
    sigma = jax.nn.sigmoid(gate)
    silu_gate = gate * sigma
    hidden_low = (silu_gate * up_proj).astype(brain_float_half)
    block_out = (
        mixed + jnp.dot(hidden_low, full_down, preferred_element_type=single_float)
    ).astype(brain_float_half)
    back_q, back_k, back_v, back_o = full_q, full_k, full_v, full_o
    back_gate, back_up, back_down, gain_back = full_gate, full_up, full_down, gain_full
    upstream = cotangent.reshape(tok_rows, width)
    grad_hidden = jnp.einsum("td,fd->tf", upstream, back_down, preferred_element_type=single_float)
    grad_gate_low = (grad_hidden * up_proj * sigma * (1.0 + gate * (1.0 - sigma))).astype(
        brain_float_half
    )
    grad_up_low = (grad_hidden * silu_gate).astype(brain_float_half)
    own_down = scatter_weight(by_columns(hidden_low, upstream, seq_ways), 2)
    own_gate = scatter_weight(by_columns(second_normed, grad_gate_low, seq_ways), 0)
    own_up = scatter_weight(by_columns(second_normed, grad_up_low, seq_ways), 1)
    grad_second = jnp.einsum(
        "tf,df->td", grad_gate_low, back_gate, preferred_element_type=single_float
    ) + jnp.einsum("tf,df->td", grad_up_low, back_up, preferred_element_type=single_float)
    grad_gain_second = jnp.sum(grad_second * second_unit, 0)
    grad_mixed = upstream.astype(single_float) + norm_back(
        grad_second, second_unit, second_rms, gain_back[1]
    )
    grad_mixed_low = grad_mixed.astype(brain_float_half)
    own_o = scatter_weight(by_columns(attn_low, grad_mixed_low, seq_ways), 1)
    gradient_attention_reduced = jnp.einsum(
        "td,cd->tc", grad_mixed_low, back_o, preferred_element_type=single_float
    ).astype(brain_float_half)
    gradient_attention_fivefold = gradient_attention_reduced.reshape(
        query_groups, slice_length, KEY_VALUE_HEADS, query_group_width, HEAD_SIZE
    )
    delta = jnp.sum(gradient_attention_fivefold.astype(single_float) * attn_nat, -1).transpose(
        0, 2, 3, 1
    )
    kv_full = sequence_segment

    def back_block(block_index, state):
        grad_query, grad_kv = state
        offset = block_index * slice_length
        sequence_segment = lax.dynamic_slice_in_dim(kv_full, offset, slice_length, 1)
        key_portion = sequence_segment[..., :key_value_width].reshape(
            query_groups, slice_length, KEY_VALUE_HEADS, HEAD_SIZE
        )
        value_portion = sequence_segment[..., key_value_width:].reshape(
            query_groups, slice_length, KEY_VALUE_HEADS, HEAD_SIZE
        )
        scores = (
            jnp.einsum(
                "sqkgd,sjkd->skgqj",
                query_fivefold,
                key_portion,
                preferred_element_type=single_float,
            )
            * 0.125
        )
        visible = (offset + jnp.arange(slice_length, dtype=jnp.int32))[None, :] <= positions[
            :, None
        ]
        probs = jnp.where(visible, jnp.exp(scores - log_total[..., None]), 0.0)
        grad_probs = jnp.einsum(
            "sqkgd,sjkd->skgqj",
            gradient_attention_fivefold,
            value_portion,
            preferred_element_type=single_float,
        )
        grad_scores = (probs * (grad_probs - delta[..., None])).astype(brain_float_half)
        grad_query = (
            grad_query
            + jnp.einsum(
                "skgqj,sjkd->sqkgd", grad_scores, key_portion, preferred_element_type=single_float
            )
            * 0.125
        )
        grad_key = (
            jnp.einsum(
                "skgqj,sqkgd->sjkd",
                grad_scores,
                query_fivefold,
                preferred_element_type=single_float,
            )
            * 0.125
        )
        grad_value = jnp.einsum(
            "skgqj,sqkgd->sjkd",
            probs.astype(brain_float_half),
            gradient_attention_fivefold,
            preferred_element_type=single_float,
        )
        term = jnp.concatenate(
            [
                grad_key.reshape(query_groups, slice_length, key_value_width),
                grad_value.reshape(query_groups, slice_length, key_value_width),
            ],
            -1,
        )
        grad_kv = lax.dynamic_update_slice_in_dim(grad_kv, term, offset, 1)
        return (grad_query, grad_kv)

    start_grads = (
        jnp.zeros(
            (query_groups, slice_length, KEY_VALUE_HEADS, query_group_width, HEAD_SIZE),
            single_float,
        ),
        jnp.zeros(kv_full.shape, single_float),
    )
    grad_query, grad_kv = lax.fori_loop(0, lax.axis_index("seq") + 1, back_block, start_grads)
    local_key_value = scatter_bits(
        grad_kv.reshape(query_groups, seq_ways, slice_length, 2 * key_value_width)
        .transpose(1, 0, 2, 3)
        .astype(brain_float_half),
        seq_places,
        seq_places,
    )
    grad_key_low = (
        inverse_rotary(
            local_key_value[..., :key_value_width].reshape(
                query_groups, slice_length, KEY_VALUE_HEADS, HEAD_SIZE
            ),
            cosine_table,
            sine_table,
        )
        .astype(brain_float_half)
        .reshape(tok_rows, key_value_width)
    )
    grad_value_low = (
        local_key_value[..., key_value_width:]
        .astype(brain_float_half)
        .reshape(tok_rows, key_value_width)
    )
    grad_query_low = (
        inverse_rotary(
            grad_query.reshape(query_groups, slice_length, QUERY_HEADS, HEAD_SIZE),
            cosine_table,
            sine_table,
        )
        .astype(brain_float_half)
        .reshape(tok_rows, QUERY_HEADS * HEAD_SIZE)
    )
    grad_first = jnp.einsum(
        "tc,dc->td", grad_query_low, back_q, preferred_element_type=single_float
    )
    grad_first = grad_first + jnp.einsum(
        "tc,dc->td", grad_key_low, back_k, preferred_element_type=single_float
    )
    grad_first = grad_first + jnp.einsum(
        "tc,dc->td", grad_value_low, back_v, preferred_element_type=single_float
    )
    grad_gain_first = jnp.sum(grad_first * first_unit, 0)
    grad_tokens = (grad_mixed + norm_back(grad_first, first_unit, first_rms, gain_back[0])).astype(
        brain_float_half
    )
    heads_packed = jnp.concatenate(
        [
            part[:, i * wide : (i + 1) * wide]
            for i in range(seq_ways)
            for part, wide in ((grad_query_low, qw), (grad_key_low, kw), (grad_value_low, kw))
        ],
        -1,
    )
    grad_heads = by_columns(first_norm_output, heads_packed, seq_ways).reshape(
        seq_ways, data_ways, shard_rows, qw + 2 * kw
    )
    grad_gains = (
        jnp.stack([grad_gain_first, grad_gain_second])
        .reshape(2, data_ways, shard_rows)
        .transpose(1, 0, 2)
    )
    grad_gains = jnp.pad(
        grad_gains, ((0, 0), (0, 6), (0, qw + 2 * kw - shard_rows))
    ).astype(brain_float_half)
    grad_heads = jnp.concatenate(
        [grad_heads, jnp.broadcast_to(grad_gains[None], (seq_ways,) + grad_gains.shape)], 2
    )
    own_heads = scatter_weight(
        grad_heads.reshape(seq_ways, data_ways * (shard_rows + 8), qw + 2 * kw), 0
    )
    owned = [
        own_heads[:shard_rows, :qw],
        own_heads[:shard_rows, qw : qw + kw],
        own_heads[:shard_rows, qw + kw :],
        own_o,
        own_gate,
        own_up,
        own_down,
    ]
    own_gains = own_heads[shard_rows : shard_rows + 2, :shard_rows]
    return (
        block_out.reshape(query_groups, slice_length, width),
        grad_tokens.reshape(query_groups, slice_length, width),
        owned[0],
        owned[1],
        owned[2],
        owned[3],
        owned[4],
        owned[5],
        owned[6],
        own_gains,
    )


def solution(mesh):
    return jax.shard_map(
        on_device,
        mesh=mesh,
        in_specs=(
            P("dp", "seq", None),
            P("dp", "seq", None),
            P("dp", "seq"),
            P("dp", "seq"),
            P("dp", "seq"),
            P("dp", "seq"),
            P("dp", "seq"),
            P("dp", "seq"),
            P("dp", "seq"),
            P(None, "dp"),
        ),
        out_specs=(
            P("dp", "seq", None),
            P("dp", "seq", None),
            P("dp", "seq"),
            P("dp", "seq"),
            P("dp", "seq"),
            P("dp", "seq"),
            P("dp", "seq"),
            P("dp", "seq"),
            P("dp", "seq"),
            P(None, "dp"),
        ),
        check_vma=False,
    )
```

```python
import jax
import jax.numpy as jnp
from jax import lax
from jax.experimental import pallas as pl
from jax.experimental.pallas import tpu as pltpu
from jax.sharding import PartitionSpec as P

QUERY_HEADS = 15
KEY_VALUE_HEADS = 5
HEAD_SIZE = 64


EPS = 1e-05
NEG = -1e30


def bit_places():
    seq_bits = lax.axis_size("seq").bit_length() - 1
    data_bits = lax.axis_size("dp").bit_length() - 1
    return [("seq", b) for b in range(seq_bits - 1, -1, -1)] + [
        ("dp", b) for b in range(data_bits - 1, -1, -1)
    ]


def exchange(values, axis, bit):
    pairs = [(i, i ^ (1 << bit)) for i in range(lax.axis_size(axis))]
    return lax.ppermute(values, axis, pairs)


def my_bit(axis, bit):
    return (lax.axis_index(axis) >> bit) & 1


def rotated(kind):
    every = bit_places()
    seq = [p for p in every if p[0] == "seq" and p[1] > 0]
    data = [p for p in every if p[0] == "dp"]
    last = [("seq", 0)]
    if kind == 0:
        return data + seq + last
    if kind == 1:
        return data[:-1] + seq + data[-1:] + last
    return data[:-2] + seq + data[-1:] + data[-2:-1] + last


def gather_bits(shard, order, places):
    current = shard.reshape((1,) * len(places) + shard.shape)
    for axis, bit in order:
        dim = places.index((axis, bit))
        other = exchange(current, axis, bit)
        high = my_bit(axis, bit) == 1
        current = jnp.concatenate(
            [jnp.where(high, other, current), jnp.where(high, current, other)], dim
        )
    return current.reshape((-1,) + shard.shape)


def gather_weight(shard, kind):
    full = gather_bits(shard, rotated(kind), bit_places())
    return full.reshape(lax.axis_size("seq"), lax.axis_size("dp"), *shard.shape)


def scatter_bits(blocks, order, places):
    payload = blocks.shape[1:]
    current = blocks.reshape((2,) * len(places) + payload)
    for axis, bit in order:
        dim = places.index((axis, bit))
        here = my_bit(axis, bit)
        send = lax.dynamic_slice_in_dim(current, 1 - here, 1, dim).astype(jnp.bfloat16)
        keep = lax.dynamic_slice_in_dim(current, here, 1, dim)
        other = exchange(send, axis, bit)
        current = keep.astype(jnp.float32) + other.astype(jnp.float32)
        if (axis, bit) != order[-1]:
            current = current.astype(jnp.bfloat16)
    return current.reshape(payload)


def scatter_weight(grad, kind):
    data_ways = lax.axis_size("dp")
    seq_ways, height, breadth = grad.shape
    blocks = grad.reshape(seq_ways * data_ways, height // data_ways, breadth)
    return scatter_bits(blocks, rotated(kind)[::-1], bit_places())


def side_by_side(blocks):
    rows = blocks.reshape(blocks.shape[0], -1, blocks.shape[3])
    return jnp.concatenate([rows[i] for i in range(blocks.shape[0])], -1)


def by_columns(left, right, seq_ways):
    wide = right.shape[1] // seq_ways
    return jnp.stack(
        [
            jnp.einsum(
                "ta,tb->ab",
                left,
                right[:, i * wide : (i + 1) * wide],
                preferred_element_type=jnp.float32,
            ).astype(jnp.bfloat16)
            for i in range(seq_ways)
        ]
    )


GROUP = QUERY_HEADS // KEY_VALUE_HEADS
KEY_WIDTH = KEY_VALUE_HEADS * HEAD_SIZE
VMEM_BYTES = 48 * 1024 * 1024


def product(left, right, left_dim, right_dim):
    return lax.dot_general(
        left, right, (((left_dim,), (right_dim,)), ((), ())), preferred_element_type=jnp.float32
    )


def head_of(ref, lead, head, base=0):
    columns = pl.ds(base + head * HEAD_SIZE, HEAD_SIZE)
    return ref[lead + (slice(None), columns)]


def below_diagonal(length):
    keys = lax.broadcasted_iota(jnp.int32, (length, length), 0)
    queries = lax.broadcasted_iota(jnp.int32, (length, length), 1)
    return keys <= queries


def attend_kernel(me_ref, q_ref, kv_ref, out_ref, log_ref, acc, best, total):
    me = me_ref[0]
    length = q_ref.shape[1]

    def block(j, diagonal):
        for kv_head in range(KEY_VALUE_HEADS):
            key = head_of(kv_ref, (j, 0), kv_head)
            value = head_of(kv_ref, (j, 0), kv_head, KEY_WIDTH)
            for head in range(kv_head * GROUP, (kv_head + 1) * GROUP):
                query = head_of(q_ref, (0,), head) * jnp.bfloat16(0.125)
                scores = product(key, query, 1, 1)
                row = pl.ds(head, 1)
                part = pl.ds(head * HEAD_SIZE, HEAD_SIZE)
                if diagonal:
                    scores = jnp.where(below_diagonal(length), scores, NEG)
                    top = jnp.max(scores, 0, keepdims=True)
                else:
                    old = best[row, :]
                    top = jnp.maximum(old, jnp.max(scores, 0, keepdims=True))
                weights = jnp.exp(scores - top)
                sums = jnp.sum(weights, 0, keepdims=True)
                term = product(value, weights.astype(jnp.bfloat16), 0, 0)
                if diagonal:
                    total[row, :] = sums
                    acc[part, :] = term
                else:
                    fade = jnp.exp(old - top)
                    total[row, :] = total[row, :] * fade + sums
                    acc[part, :] = acc[part, :] * fade + term
                best[row, :] = top

    block(me, True)

    def step(j, carry):
        block(j, False)
        return carry

    lax.fori_loop(0, me, step, 0)
    for head in range(QUERY_HEADS):
        row = pl.ds(head, 1)
        part = pl.ds(head * HEAD_SIZE, HEAD_SIZE)
        sums = total[row, :]
        log_ref[0, row, :] = best[row, :] + jnp.log(sums)
        out_ref[0, :, part] = (acc[part, :] / sums).T


def attend_back_kernel(
    me_ref, q_ref, kv_ref, grad_ref, log_ref, delta_ref, grad_q_ref, grad_kv_ref, acc
):
    me = me_ref[0]
    length = q_ref.shape[1]

    def block(j, diagonal):
        for kv_head in range(KEY_VALUE_HEADS):
            key = head_of(kv_ref, (j, 0), kv_head)
            value = head_of(kv_ref, (j, 0), kv_head, KEY_WIDTH)
            grad_key = jnp.zeros((length, HEAD_SIZE), jnp.float32)
            grad_value = jnp.zeros((length, HEAD_SIZE), jnp.float32)
            for head in range(kv_head * GROUP, (kv_head + 1) * GROUP):
                query = head_of(q_ref, (0,), head) * jnp.bfloat16(0.125)
                upstream = head_of(grad_ref, (0,), head)
                row = pl.ds(head, 1)
                part = pl.ds(head * HEAD_SIZE, HEAD_SIZE)
                scores = product(key, query, 1, 1)
                if diagonal:
                    scores = jnp.where(below_diagonal(length), scores, NEG)
                probs = jnp.exp(scores - log_ref[0, row, :])
                grad_probs = product(value, upstream, 1, 1)
                grad_scores = (probs * (grad_probs - delta_ref[0, row, :])).astype(jnp.bfloat16)
                grad_value += product(probs.astype(jnp.bfloat16), upstream, 1, 0)
                grad_key += product(grad_scores, query, 1, 0)
                term = product(key, grad_scores, 0, 0)
                if diagonal:
                    acc[part, :] = term
                else:
                    acc[part, :] += term
            base = kv_head * HEAD_SIZE
            grad_kv_ref[j, 0, :, pl.ds(base, HEAD_SIZE)] = grad_key.astype(jnp.bfloat16)
            grad_kv_ref[j, 0, :, pl.ds(KEY_WIDTH + base, HEAD_SIZE)] = grad_value.astype(
                jnp.bfloat16
            )

    block(me, True)

    def step(j, carry):
        block(j, False)
        return carry

    def clear(j, carry):
        grad_kv_ref[j] = jnp.zeros(grad_kv_ref.shape[1:], jnp.bfloat16)
        return carry

    lax.fori_loop(0, me, step, 0)
    lax.fori_loop(me + 1, kv_ref.shape[0], clear, 0)
    for head in range(QUERY_HEADS):
        part = pl.ds(head * HEAD_SIZE, HEAD_SIZE)
        grad_q_ref[0, :, part] = acc[part, :].T * 0.125


def per_sequence(shape):
    rest = len(shape) - 1
    return pl.BlockSpec((1,) + tuple(shape[1:]), lambda s: (s,) + (0,) * rest)


def per_slices(shape):
    return pl.BlockSpec((shape[0], 1) + tuple(shape[2:]), lambda s: (0, s, 0, 0))


def attention(me, query, key_value):
    count, length, width = query.shape
    stats = (count, QUERY_HEADS, length)
    work = count * QUERY_HEADS * length * length * key_value.shape[0] // 2
    return pl.pallas_call(
        attend_kernel,
        grid=(count,),
        in_specs=[
            pl.BlockSpec(memory_space=pltpu.SMEM),
            per_sequence(query.shape),
            per_slices(key_value.shape),
        ],
        out_specs=[per_sequence(query.shape), per_sequence(stats)],
        out_shape=[
            jax.ShapeDtypeStruct(query.shape, jnp.float32),
            jax.ShapeDtypeStruct(stats, jnp.float32),
        ],
        scratch_shapes=[
            pltpu.VMEM((width, length), jnp.float32),
            pltpu.VMEM((QUERY_HEADS, length), jnp.float32),
            pltpu.VMEM((QUERY_HEADS, length), jnp.float32),
        ],
        compiler_params=pltpu.CompilerParams(vmem_limit_bytes=VMEM_BYTES),
        cost_estimate=pl.CostEstimate(
            flops=work * 256 * 4, bytes_accessed=16 * query.size, transcendentals=work
        ),
    )(me, query, key_value)


def attention_back(me, query, key_value, upstream, log_total, delta):
    count, length, width = query.shape
    work = count * QUERY_HEADS * length * length * key_value.shape[0] // 2
    return pl.pallas_call(
        attend_back_kernel,
        grid=(count,),
        in_specs=[
            pl.BlockSpec(memory_space=pltpu.SMEM),
            per_sequence(query.shape),
            per_slices(key_value.shape),
            per_sequence(query.shape),
            per_sequence(log_total.shape),
            per_sequence(log_total.shape),
        ],
        out_specs=[per_sequence(query.shape), per_slices(key_value.shape)],
        out_shape=[
            jax.ShapeDtypeStruct(query.shape, jnp.float32),
            jax.ShapeDtypeStruct(key_value.shape, jnp.bfloat16),
        ],
        scratch_shapes=[pltpu.VMEM((width, length), jnp.float32)],
        compiler_params=pltpu.CompilerParams(vmem_limit_bytes=VMEM_BYTES),
        cost_estimate=pl.CostEstimate(
            flops=work * 640 * 4, bytes_accessed=24 * query.size, transcendentals=work
        ),
    )(me, query, key_value, upstream, log_total, delta)


def rope_tables(positions):
    half_dim = HEAD_SIZE // 2
    freq_index = jnp.arange(half_dim).astype(jnp.float32)
    inverse = 10000.0 ** (-2.0 * freq_index / HEAD_SIZE)
    angles = positions.astype(jnp.float32)[:, None] * inverse[None, :]
    return (jnp.cos(angles), jnp.sin(angles))


def apply_rotary(values, cosine_table, sine_table):
    half_dim = values.shape[-1] // 2
    first_half = values[..., :half_dim]
    second_half = values[..., half_dim:]
    cos_wide = cosine_table[:, None, :]
    sin_wide = sine_table[:, None, :]
    return jnp.concatenate(
        [
            first_half * cos_wide - second_half * sin_wide,
            second_half * cos_wide + first_half * sin_wide,
        ],
        -1,
    )


def inverse_rotary(grads, cosine_table, sine_table):
    half_dim = grads.shape[-1] // 2
    first_half = grads[..., :half_dim]
    second_half = grads[..., half_dim:]
    cos_wide = cosine_table[:, None, :]
    sin_wide = sine_table[:, None, :]
    return jnp.concatenate(
        [
            first_half * cos_wide + second_half * sin_wide,
            second_half * cos_wide - first_half * sin_wide,
        ],
        -1,
    )


def norm_back(grad_norm, unit, inv_rms, gain_row):
    scaled = grad_norm * gain_row
    return inv_rms * (scaled - unit * jnp.mean(scaled * unit, -1, keepdims=True))


def on_device(tokens, cotangent, wq, wk, wv, wo, w_gate, w_up, w_down, gains):
    data_ways = lax.axis_size("dp")
    seq_ways = lax.axis_size("seq")
    query_groups, slice_length, width = tokens.shape
    tok_rows = query_groups * slice_length
    key_value_width = KEY_VALUE_HEADS * HEAD_SIZE
    single_float = jnp.float32
    brain_float_half = jnp.bfloat16
    seq_places = [p for p in bit_places() if p[0] == "seq"]
    shard_rows = wq.shape[0]
    qw, kw = wq.shape[1], wk.shape[1]
    packed = jnp.concatenate(
        [
            jnp.concatenate([wq, wk, wv], -1),
            jnp.pad(gains, ((0, 6), (0, qw + 2 * kw - gains.shape[1]))),
        ],
        0,
    )
    qkv_blocks = gather_weight(packed, 0)
    full_o = side_by_side(gather_weight(wo, 1))
    gate_blocks = gather_weight(w_gate, 0)
    up_blocks = gather_weight(w_up, 1)
    full_gate = side_by_side(gate_blocks)
    full_up = side_by_side(up_blocks)
    full_down = side_by_side(gather_weight(w_down, 2))
    full_q = side_by_side(qkv_blocks[:, :, :shard_rows, :qw])
    full_k = side_by_side(qkv_blocks[:, :, :shard_rows, qw : qw + kw])
    full_v = side_by_side(qkv_blocks[:, :, :shard_rows, qw + kw :])
    gain_full = (
        qkv_blocks[0, :, shard_rows : shard_rows + 2, : gains.shape[1]]
        .transpose(1, 0, 2)
        .reshape(2, width)
        .astype(single_float)
    )
    inputs = tokens.astype(single_float).reshape(tok_rows, width)
    first_rms = lax.rsqrt(jnp.mean(inputs * inputs, -1, keepdims=True) + EPS)
    first_unit = inputs * first_rms
    first_norm_output = (first_unit * gain_full[0]).astype(brain_float_half)
    query = jnp.dot(first_norm_output, full_q, preferred_element_type=single_float)
    key_projected = jnp.dot(first_norm_output, full_k, preferred_element_type=single_float)
    value_proj = jnp.dot(first_norm_output, full_v, preferred_element_type=single_float)
    positions = lax.axis_index("seq") * slice_length + jnp.arange(slice_length, dtype=jnp.int32)
    cosine_table, sine_table = rope_tables(positions)
    query_rotated = apply_rotary(
        query.reshape(query_groups, slice_length, QUERY_HEADS, HEAD_SIZE), cosine_table, sine_table
    ).astype(brain_float_half)
    key_rotated = apply_rotary(
        key_projected.reshape(query_groups, slice_length, KEY_VALUE_HEADS, HEAD_SIZE),
        cosine_table,
        sine_table,
    ).astype(brain_float_half)
    value_reduced = value_proj.astype(brain_float_half).reshape(
        query_groups, slice_length, key_value_width
    )
    key_value = jnp.concatenate(
        [key_rotated.reshape(query_groups, slice_length, key_value_width), value_reduced], -1
    )
    query_rotated = query_rotated.reshape(query_groups, slice_length, width)
    me = lax.axis_index("seq").astype(jnp.int32).reshape(1)
    kv_full = gather_bits(key_value, seq_places[::-1], seq_places)
    attn, log_total = attention(me, query_rotated, kv_full)
    attn_low = attn.reshape(tok_rows, width).astype(brain_float_half)
    mixed = inputs + jnp.dot(attn_low, full_o, preferred_element_type=single_float)
    second_rms = lax.rsqrt(jnp.mean(mixed * mixed, -1, keepdims=True) + EPS)
    second_unit = mixed * second_rms
    second_normed = (second_unit * gain_full[1]).astype(brain_float_half)
    gate = jnp.dot(second_normed, full_gate, preferred_element_type=single_float)
    up_proj = jnp.dot(second_normed, full_up, preferred_element_type=single_float)
    sigma = jax.nn.sigmoid(gate)
    silu_gate = gate * sigma
    hidden_low = (silu_gate * up_proj).astype(brain_float_half)
    block_out = (
        mixed + jnp.dot(hidden_low, full_down, preferred_element_type=single_float)
    ).astype(brain_float_half)
    back_q, back_k, back_v, back_o = full_q, full_k, full_v, full_o
    back_gate, back_up, back_down, gain_back = full_gate, full_up, full_down, gain_full
    upstream = cotangent.reshape(tok_rows, width)
    grad_hidden = jnp.einsum("td,fd->tf", upstream, back_down, preferred_element_type=single_float)
    grad_gate_low = (grad_hidden * up_proj * sigma * (1.0 + gate * (1.0 - sigma))).astype(
        brain_float_half
    )
    grad_up_low = (grad_hidden * silu_gate).astype(brain_float_half)
    own_down = scatter_weight(by_columns(hidden_low, upstream, seq_ways), 2)
    own_gate = scatter_weight(by_columns(second_normed, grad_gate_low, seq_ways), 0)
    own_up = scatter_weight(by_columns(second_normed, grad_up_low, seq_ways), 1)
    grad_second = jnp.einsum(
        "tf,df->td", grad_gate_low, back_gate, preferred_element_type=single_float
    ) + jnp.einsum("tf,df->td", grad_up_low, back_up, preferred_element_type=single_float)
    grad_gain_second = jnp.sum(grad_second * second_unit, 0)
    grad_mixed = upstream.astype(single_float) + norm_back(
        grad_second, second_unit, second_rms, gain_back[1]
    )
    grad_mixed_low = grad_mixed.astype(brain_float_half)
    own_o = scatter_weight(by_columns(attn_low, grad_mixed_low, seq_ways), 1)
    gradient_attention_reduced = jnp.einsum(
        "td,cd->tc", grad_mixed_low, back_o, preferred_element_type=single_float
    ).astype(brain_float_half)
    upstream_heads = gradient_attention_reduced.reshape(query_groups, slice_length, width)
    delta = (
        jnp.sum(
            (upstream_heads.astype(single_float) * attn).reshape(
                query_groups, slice_length, QUERY_HEADS, HEAD_SIZE
            ),
            -1,
        )
    ).transpose(0, 2, 1)
    grad_query, grad_kv = attention_back(
        me, query_rotated, kv_full, upstream_heads, log_total, delta
    )
    local_key_value = scatter_bits(grad_kv, seq_places, seq_places)
    grad_key_low = (
        inverse_rotary(
            local_key_value[..., :key_value_width].reshape(
                query_groups, slice_length, KEY_VALUE_HEADS, HEAD_SIZE
            ),
            cosine_table,
            sine_table,
        )
        .astype(brain_float_half)
        .reshape(tok_rows, key_value_width)
    )
    grad_value_low = (
        local_key_value[..., key_value_width:]
        .astype(brain_float_half)
        .reshape(tok_rows, key_value_width)
    )
    grad_query_low = (
        inverse_rotary(
            grad_query.reshape(query_groups, slice_length, QUERY_HEADS, HEAD_SIZE),
            cosine_table,
            sine_table,
        )
        .astype(brain_float_half)
        .reshape(tok_rows, QUERY_HEADS * HEAD_SIZE)
    )
    grad_first = jnp.einsum(
        "tc,dc->td", grad_query_low, back_q, preferred_element_type=single_float
    )
    grad_first = grad_first + jnp.einsum(
        "tc,dc->td", grad_key_low, back_k, preferred_element_type=single_float
    )
    grad_first = grad_first + jnp.einsum(
        "tc,dc->td", grad_value_low, back_v, preferred_element_type=single_float
    )
    grad_gain_first = jnp.sum(grad_first * first_unit, 0)
    grad_tokens = (grad_mixed + norm_back(grad_first, first_unit, first_rms, gain_back[0])).astype(
        brain_float_half
    )
    heads_packed = jnp.concatenate(
        [
            part[:, i * wide : (i + 1) * wide]
            for i in range(seq_ways)
            for part, wide in ((grad_query_low, qw), (grad_key_low, kw), (grad_value_low, kw))
        ],
        -1,
    )
    grad_heads = by_columns(first_norm_output, heads_packed, seq_ways).reshape(
        seq_ways, data_ways, shard_rows, qw + 2 * kw
    )
    grad_gains = (
        jnp.stack([grad_gain_first, grad_gain_second])
        .reshape(2, data_ways, shard_rows)
        .transpose(1, 0, 2)
    )
    grad_gains = jnp.pad(
        grad_gains, ((0, 0), (0, 6), (0, qw + 2 * kw - shard_rows))
    ).astype(brain_float_half)
    grad_heads = jnp.concatenate(
        [grad_heads, jnp.broadcast_to(grad_gains[None], (seq_ways,) + grad_gains.shape)], 2
    )
    own_heads = scatter_weight(
        grad_heads.reshape(seq_ways, data_ways * (shard_rows + 8), qw + 2 * kw), 0
    )
    owned = [
        own_heads[:shard_rows, :qw],
        own_heads[:shard_rows, qw : qw + kw],
        own_heads[:shard_rows, qw + kw :],
        own_o,
        own_gate,
        own_up,
        own_down,
    ]
    own_gains = own_heads[shard_rows : shard_rows + 2, :shard_rows]
    return (
        block_out.reshape(query_groups, slice_length, width),
        grad_tokens.reshape(query_groups, slice_length, width),
        owned[0],
        owned[1],
        owned[2],
        owned[3],
        owned[4],
        owned[5],
        owned[6],
        own_gains,
    )


def solution(mesh):
    return jax.shard_map(
        on_device,
        mesh=mesh,
        in_specs=(
            P("dp", "seq", None),
            P("dp", "seq", None),
            P("dp", "seq"),
            P("dp", "seq"),
            P("dp", "seq"),
            P("dp", "seq"),
            P("dp", "seq"),
            P("dp", "seq"),
            P("dp", "seq"),
            P(None, "dp"),
        ),
        out_specs=(
            P("dp", "seq", None),
            P("dp", "seq", None),
            P("dp", "seq"),
            P("dp", "seq"),
            P("dp", "seq"),
            P("dp", "seq"),
            P("dp", "seq"),
            P("dp", "seq"),
            P("dp", "seq"),
            P(None, "dp"),
        ),
        check_vma=False,
    )
```
